32 devices in a mesh: row: 4 (over x, core), col: 8 (over z, y).
Axes of the slice: x: 2, y: 2, z: 4, core: 2. Of those that a mesh axis runs over, the one named last changes fastest.
Arguments:
- send_cells: int32 [32, 32, 512], P(('row', 'col')), may hold values from 0 to 65535, as said below
- send_species: int32 [32, 32, 512], P(('row', 'col')), may hold values from 0 to 5
- send_mix: bfloat16 [32, 6, 32, 512], P(('row', 'col')), may hold values from 0 to 0.5
- send_counts: int32 [32, 32], P(('row', 'col')), may hold values from 64 to 512, as said below
- chi: float32 [6, 6], replicated, may hold values from 0 to 8
Outputs:
- forces: float32 [32, 3, 32, 512], P(('row', 'col'))
The draws below stay inside these ranges and needn't reach their ends.
Inputs may be any that keep to these rules, and one draw needn't show every extreme that they name: `send_cells`: local cell (x * 16 + y) * 256 + z in the destination brick; domain s (flat index) holds particles with z from s * 8 to (s + 1) * 8 - 1 only. `send_counts`: slots at or beyond the count are unused. At most 512 particles go from one domain to one brick; in every draw some domain fills a slot list, and one brick receives 512 from every domain.
All inputs are finite; a program needn't handle non-finite values.
Results may differ from the reference program's by a relative error of at most 0.0023.
Values may be sent and summed in bfloat16 or wider, within the bound.
A program may use at most 256 MiB of HBM per device.

```python
import jax
import jax.numpy as jnp
from jax import lax

SPECIES = 6
BX = 16
BY = 16
NZ = 256
SLOTS = 512
DOMAINS = 32
NX = 64
NY = 128
N_COL = 8


def draw_send_counts(key, part):
    key_heavy, key_light, key_full = jax.random.split(jax.random.fold_in(key, 11), 3)
    source = jnp.arange(DOMAINS, dtype=jnp.int32)[:, None]
    heavy = jnp.abs(2 * source - DOMAINS + 1) < DOMAINS // 2
    heavy_counts = jax.random.randint(key_heavy, (DOMAINS, DOMAINS), SLOTS // 2, SLOTS + 1)
    light_counts = jax.random.randint(key_light, (DOMAINS, DOMAINS), SLOTS // 8, SLOTS // 2 + 1)
    counts = jnp.where(heavy, heavy_counts, light_counts)
    full_brick = jax.random.randint(key_full, (), 0, DOMAINS)
    counts = jnp.where(jnp.arange(DOMAINS, dtype=jnp.int32)[None, :] == full_brick, SLOTS, counts)
    return counts.astype(jnp.int32)


def draw_send_cells(key, part):
    key_x, key_y, key_z = jax.random.split(jax.random.fold_in(key, 23), 3)
    shape = (DOMAINS, DOMAINS, SLOTS)
    cell_x = jax.random.randint(key_x, shape, 0, BX)
    cell_y = jax.random.randint(key_y, shape, 0, BY)
    offset = jax.random.randint(key_z, shape, 0, NZ // DOMAINS)
    source = jnp.arange(DOMAINS, dtype=jnp.int32)[:, None, None]
    cell_z = source * (NZ // DOMAINS) + offset
    return ((cell_x * BY + cell_y) * NZ + cell_z).astype(jnp.int32)


def set_ends(entries, stream_key, low, high):
    shape = entries.shape
    spot = [jax.random.randint(jax.random.fold_in(stream_key, axis), (), 0, shape[axis]) for axis in range(len(shape))]
    entries = entries.at[tuple(spot)].set(low)
    longest = shape.index(max(shape))
    spot[longest] = (spot[longest] + 1) % shape[longest]
    return entries.at[tuple(spot)].set(high)


def level_of(rng, extent, cuts, smallest, largest):
    factor_of, own = 1.0, jax.random.fold_in(rng, 6)
    for position, shards_of in cuts:
        heights = jnp.exp(jax.random.uniform(jax.random.fold_in(own, position), (shards_of,), jnp.float32, smallest / len(cuts), largest / len(cuts)))
        factor_of = factor_of * jnp.repeat(heights, extent[position] // shards_of).reshape([-1 if axis == position else 1 for axis in range(len(extent))])
    return factor_of


def setup_inputs(seed: int = 0) -> dict:
    key_of = jax.random.split(jax.random.key(seed), 6)
    return {
        "send_cells": draw_send_cells(jax.random.fold_in(key_of[5], 71), 0),
        "send_species": set_ends(jax.random.randint(key_of[1], (DOMAINS, DOMAINS, SLOTS), 0, SPECIES), jax.random.fold_in(key_of[1], 1), 0, SPECIES - 1).astype(jnp.int32),
        "send_mix": jnp.clip(0.5 * jax.random.uniform(key_of[2], (DOMAINS, SPECIES, DOMAINS, SLOTS), jnp.float32) ** level_of(key_of[2], (DOMAINS, SPECIES, DOMAINS, SLOTS), ((0, 32),), -0.2, 0.2), 0.0, 0.5).astype(jnp.bfloat16),
        "send_counts": draw_send_counts(jax.random.fold_in(key_of[5], 71), 0),
        "chi": jnp.clip(jax.random.uniform(key_of[4], (SPECIES, SPECIES), jnp.float32, 0.0, 8.0), 0.0, 8.0),
    }


raw_taps = (0.1353352832366127, 0.6065306597126334, 1.0, 0.6065306597126334, 0.1353352832366127)
tap_total = sum(raw_taps)
taps = tuple(t / tap_total for t in raw_taps)
rho_ref = 2.0
inv_kappa = 1.0


def smooth(padded):
    width_x = padded.shape[1] - 4
    width_y = padded.shape[2] - 4
    along_x = taps[0] * padded[:, 0:width_x]
    for t in range(1, 5):
        along_x = along_x + taps[t] * padded[:, t:t + width_x]
    along_y = taps[0] * along_x[:, :, 0:width_y]
    for t in range(1, 5):
        along_y = along_y + taps[t] * along_x[:, :, t:t + width_y]
    along_z = taps[0] * jnp.roll(along_y, 2, axis=3)
    for t in range(1, 5):
        along_z = along_z + taps[t] * jnp.roll(along_y, 2 - t, axis=3)
    return along_z


def potential_of(filtered, chi):
    count = chi.shape[0]
    chis = 0.5 * (chi + chi.T) * (1.0 - jnp.eye(count, dtype=jnp.float32))
    mixing = jnp.einsum("kl,lxyz->kxyz", chis, filtered, precision=lax.Precision.HIGHEST) / rho_ref
    total = jnp.sum(filtered, axis=0) / rho_ref
    return mixing + inv_kappa * (total[None] - 1.0)


def reference(send_cells, send_species, send_mix, send_counts, chi):
    slot_ids = jnp.arange(SLOTS, dtype=jnp.int32)
    valid = slot_ids[None, None, :] < send_counts[:, :, None]
    onehot = (send_species[:, None, :, :] == jnp.arange(SPECIES, dtype=jnp.int32)[None, :, None, None]).astype(jnp.float32)
    weights = jnp.where(valid[:, None], onehot + send_mix.astype(jnp.float32), 0.0).astype(jnp.bfloat16)
    dest = jnp.arange(DOMAINS, dtype=jnp.int32)[None, :, None]
    brick_r = dest // N_COL
    brick_q = dest % N_COL
    cell_x = send_cells // (BY * NZ)
    cell_y = (send_cells // NZ) % BY
    cell_z = send_cells % NZ
    place = ((brick_r * BX + cell_x) * NY + brick_q * BY + cell_y) * NZ + cell_z
    place = place.reshape(-1).astype(jnp.int32)
    flat_w = jnp.transpose(weights.astype(jnp.float32), (1, 0, 2, 3)).reshape(SPECIES, -1)
    density = jnp.zeros((SPECIES, NX * NY * NZ), jnp.float32).at[:, place].add(flat_w)
    density = density.reshape(SPECIES, NX, NY, NZ)
    padded = jnp.pad(density, ((0, 0), (2, 2), (2, 2), (0, 0)), mode="wrap")
    filtered = smooth(padded)
    potential = potential_of(filtered, chi)
    extended = jnp.pad(potential, ((0, 0), (1, 1), (1, 1), (0, 0)), mode="wrap")
    grad_x = 0.5 * (extended[:, 2:, 1:-1] - extended[:, :-2, 1:-1])
    grad_y = 0.5 * (extended[:, 1:-1, 2:] - extended[:, 1:-1, :-2])
    grad_z = 0.5 * (jnp.roll(potential, -1, axis=3) - jnp.roll(potential, 1, axis=3))
    results = []
    for grad in (grad_x, grad_y, grad_z):
        picked = grad.reshape(SPECIES, -1)[:, place]
        results.append((-jnp.sum(flat_w * picked, axis=0)).reshape(DOMAINS, DOMAINS, SLOTS))
    return jnp.stack(results, axis=1)
```

```python
import functools

import jax
import jax.numpy as jnp
import numpy as np
from jax import lax
from jax.experimental import pallas as pl
from jax.experimental.pallas import tpu as pltpu
from jax.sharding import PartitionSpec as P

BX = 16
BY = 16
NZ = 256
LANES = 128
HALF = LANES // BY
REACH = 3

raw_taps = (0.1353352832366127, 0.6065306597126334, 1.0, 0.6065306597126334, 0.1353352832366127)
tap_total = sum(raw_taps)
taps = tuple(t / tap_total for t in raw_taps)
rho_ref = 2.0
inv_kappa = 1.0


def pieces_of(band):
    out = []
    hop, left = 1, REACH
    while left > 0:
        n = min(band, left)
        out.append((hop, band - n, n, -(hop - 1) * band - n))
        out.append((-hop, 0, n, hop * band))
        left -= n
        hop += 1
    return out


def constants_of(species, band):
    pieces = pieces_of(band)
    rows_d = species * band
    picked = [(k, first + p) for _, first, n, _ in pieces for k in range(species) for p in range(n)]
    pick = np.zeros((-(-len(picked) // 8) * 8, rows_d), np.float32)
    for i, (k, z) in enumerate(picked):
        pick[i, k * band + z] = 1.0
    source = [(k, z) for k in range(species) for z in range(band)]
    source += [(k, at + p) for _, _, n, at in pieces for k in range(species) for p in range(n)]
    rows_v = -(-len(source) // 16) * 16
    left = np.zeros((2 * rows_d, species), np.float32)
    right = np.zeros((species, rows_v), np.float32)
    along_z = np.zeros((2 * rows_d, rows_v), np.float32)
    off_diag = np.zeros((2 * rows_d, rows_v), np.float32)
    tap = lambda t: taps[t + 2] if -2 <= t <= 2 else 0.0
    for kind in range(2):
        for k in range(species):
            for z in range(band):
                i = kind * rows_d + k * band + z
                left[i, k] = 1.0
                for j, (l, at) in enumerate(source):
                    right[l, j] = 1.0
                    off_diag[i, j] = float(k != l)
                    value = tap(at - z) if kind == 0 else tap(at - z - 1) - tap(at - z + 1)
                    along_z[i, j] = -0.5 * value
    return pick.astype(jnp.bfloat16), left, right, along_z, off_diag


def exact(a, b, dims=(((1,), (0,)), ((), ()))):
    return lax.dot_general(a, b, dims, precision=lax.Precision.HIGHEST, preferred_element_type=jnp.float32)


def fill_weights(species_ref, mix_ref, wts):
    for k in range(wts.shape[0]):
        onehot = (species_ref[0] == k).astype(jnp.float32)
        wts[k] = (onehot + mix_ref[0, k].astype(jnp.float32)).astype(jnp.bfloat16).astype(jnp.float32)


def banded_of(cells, count, wts, d, first_z, band):
    slots = cells.shape[1]
    z = (cells & (NZ - 1)) - first_z
    z = jnp.where(lax.broadcasted_iota(jnp.int32, (1, slots), 1) < count, z, -1)
    hit = z == lax.broadcasted_iota(jnp.int32, (band, slots), 0)
    parts = [jnp.where(hit, wts[k, pl.ds(d, 1), :], 0.0) for k in range(wts.shape[0])]
    return jnp.concatenate(parts, axis=0)


def table_of(cells):
    plane = lax.shift_right_logical(cells, NZ.bit_length() - 1)
    ids = lax.broadcasted_iota(jnp.int32, (BX * BY, cells.shape[1]), 0)
    return jnp.where(plane == ids, 1.0, 0.0).astype(jnp.bfloat16)


def deposit_kernel(n_col, band, first_ref, counts_ref, cells_ref, species_ref, mix_ref, pick_ref, *refs):
    pieces = pieces_of(band)
    dens_ref, sends, stages, wts = refs[0], refs[1:1 + len(pieces)], refs[1 + len(pieces):1 + 2 * len(pieces)], refs[-1]
    count = wts.shape[0]
    fill_weights(species_ref, mix_ref, wts)
    first_z = first_ref[0]

    def one_row(r, carry):
        for q in range(n_col):
            d = r * n_col + q
            cells = cells_ref[0, pl.ds(d, 1), :]
            banded = banded_of(cells, counts_ref[0, d], wts, d, first_z, band)
            tile = lax.dot_general(
                banded.astype(jnp.bfloat16), table_of(cells), (((1,), (1,)), ((), ())),
                preferred_element_type=jnp.float32,
            )
            dens_ref[2 * r, q] = tile[:, :LANES]
            dens_ref[2 * r + 1, q] = tile[:, LANES:]
            edge = jnp.dot(pick_ref[...], tile.astype(jnp.bfloat16), preferred_element_type=jnp.float32)
            at = 0
            for stage, (_, _, n, _) in zip(stages, pieces):
                rows = n * count
                stage[q * rows:(q + 1) * rows, :] = edge[at:at + rows]
                at += rows
        for send, stage in zip(sends, stages):
            send[r] = stage[...].astype(jnp.bfloat16)
        return carry

    lax.fori_loop(0, dens_ref.shape[0] // 2, one_row, 0)


def lane_of(rows):
    return lax.broadcasted_iota(jnp.int32, (rows, LANES), 1)


def roll(value, shift):
    return pltpu.roll(value, shift % LANES, 1)


def moved_y(before, here, after, lane_y, t):
    if t > 0:
        return jnp.where(lane_y < BY - t, roll(here, -t), roll(after, BY - t))
    return jnp.where(lane_y >= -t, roll(here, -t), roll(before, -BY - t))


def moved_x(before, here, after, lane_x, t):
    if t > 0:
        return jnp.where(lane_x < HALF - t, roll(here, -t * BY), roll(after, -t * BY))
    return jnp.where(lane_x >= -t, roll(here, -t * BY), roll(before, -t * BY))


def smoothed(moved, before, here, after, lane):
    total = taps[2] * here
    for t in (1, 2):
        total = total + taps[2 + t] * (moved(before, here, after, lane, t) + moved(before, here, after, lane, -t))
    return total


def force_kernel(n_col, band, first_ref, counts_ref, cells_ref, species_ref, mix_ref, chi_ref, left_ref, right_ref,
                 along_ref, off_ref, dens_ref, *refs):
    pieces = pieces_of(band)
    recvs = refs[:len(pieces)]
    out_ref, wts, raw, half_done, fields, maps = refs[len(pieces):]
    count = wts.shape[0]
    rows_d = count * band
    halves, rows_v = raw.shape[0], raw.shape[2]
    rows_m = maps.shape[1]
    first_z = first_ref[0]
    fill_weights(species_ref, mix_ref, wts)

    chi = chi_ref[...]
    mixing = exact(exact(left_ref[...], chi), right_ref[...])
    mixing += exact(exact(left_ref[...], chi, (((1,), (1,)), ((), ()))), right_ref[...])
    mixing = (mixing * (0.5 / rho_ref)) * off_ref[...] + inv_kappa / rho_ref
    full = mixing * along_ref[...]
    high = full.astype(jnp.bfloat16)
    maps[:2 * rows_d] = high
    maps[2 * rows_d:] = (full - high.astype(jnp.float32)).astype(jnp.bfloat16)

    def spread(r, carry):
        got = [recv[r].astype(jnp.float32) for recv in recvs]
        for q in range(n_col):
            parts = [part[q * n * count:(q + 1) * n * count] for part, (_, _, n, _) in zip(got, pieces)]
            used = rows_d + 2 * REACH * count
            edge = jnp.concatenate(parts, axis=0)
            for h in range(2):
                raw[2 * r + h, q, :rows_d] = dens_ref[2 * r + h, q]
                raw[2 * r + h, q, rows_d:used] = edge[:, h * LANES:(h + 1) * LANES]
                if rows_v > used:
                    raw[2 * r + h, q, used:] = jnp.zeros((rows_v - used, LANES), jnp.float32)
        return carry

    lax.fori_loop(0, halves // 2, spread, 0)

    def smooth_y(i, carry):
        h, q = i // n_col, i % n_col
        lane = lane_of(rows_v) % BY
        half_done[h, q] = smoothed(
            moved_y, raw[h, (q + n_col - 1) % n_col], raw[h, q], raw[h, (q + 1) % n_col], lane
        )
        return carry

    lax.fori_loop(0, halves * n_col, smooth_y, 0)

    def smooth_x(i, carry):
        r, q = i // n_col, i % n_col
        lane = lane_of(rows_v) // BY
        a, b = half_done[(2 * r + halves - 1) % halves, q], half_done[2 * r, q]
        c, d = half_done[2 * r + 1, q], half_done[(2 * r + 2) % halves, q]
        value = jnp.concatenate(
            [smoothed(moved_x, a, b, c, lane), smoothed(moved_x, b, c, d, lane)], axis=1
        )
        if rows_m > rows_v:
            value = jnp.concatenate([value, jnp.zeros((rows_m - rows_v, 2 * LANES), jnp.float32)], axis=0)
        top = value.astype(jnp.bfloat16)
        rest = (value - top.astype(jnp.float32)).astype(jnp.bfloat16)
        first = jnp.dot(maps[...], top, preferred_element_type=jnp.float32)
        field = first[:2 * rows_d] + first[2 * rows_d:]
        field = field + jnp.dot(maps[:2 * rows_d], rest, preferred_element_type=jnp.float32)
        fields[2 * r, q] = field[:, :LANES]
        fields[2 * r + 1, q] = field[:, LANES:]
        return carry

    lax.fori_loop(0, halves // 2 * n_col, smooth_x, 0)

    def gather(d, carry):
        r, q = d // n_col, d % n_col
        lane = lane_of(rows_d)
        lane_x, lane_y = lane // BY, lane % BY
        parts = []
        for h in range(2):
            at = 2 * r + h
            here = fields[at, q, :rows_d]
            back, on = fields[(at + halves - 1) % halves, q, :rows_d], fields[(at + 1) % halves, q, :rows_d]
            grad_x = moved_x(back, here, on, lane_x, 1) - moved_x(back, here, on, lane_x, -1)
            back, on = fields[at, (q + n_col - 1) % n_col, :rows_d], fields[at, (q + 1) % n_col, :rows_d]
            grad_y = moved_y(back, here, on, lane_y, 1) - moved_y(back, here, on, lane_y, -1)
            parts.append((grad_x, grad_y, fields[at, q, rows_d:]))
        cells = cells_ref[0, pl.ds(d, 1), :]
        table = table_of(cells)
        banded = banded_of(cells, counts_ref[0, d], wts, d, first_z, band)
        for a in range(3):
            grad = jnp.concatenate([parts[0][a], parts[1][a]], axis=1)
            top = grad.astype(jnp.bfloat16)
            rest = (grad - top.astype(jnp.float32)).astype(jnp.bfloat16)
            value = jnp.dot(top, table, preferred_element_type=jnp.float32)
            value = value + jnp.dot(rest, table, preferred_element_type=jnp.float32)
            out_ref[0, a, pl.ds(d, 1), :] = jnp.sum(value * banded, axis=0, keepdims=True)
        return carry

    lax.fori_loop(0, halves // 2 * n_col, gather, 0)


def body(n_row, n_col, send_cells, send_species, send_mix, send_counts, chi):
    species, domains, slots = send_mix.shape[1:]
    band = NZ // domains
    halves = 2 * n_row
    rows_d = species * band
    pieces = pieces_of(band)
    pick, left, right, along_z, off_diag = constants_of(species, band)
    rows_v = -(-(rows_d + 2 * REACH * species) // 8) * 8
    first = ((lax.axis_index("row") * n_col + lax.axis_index("col")) * band).astype(jnp.int32)[None]
    smem, vmem = pl.BlockSpec(memory_space=pltpu.SMEM), pl.BlockSpec(memory_space=pltpu.VMEM)
    params = pltpu.CompilerParams(vmem_limit_bytes=48 * 2**20)
    edge_rows = [n_col * n * species for _, _, n, _ in pieces]
    made = pl.pallas_call(
        functools.partial(deposit_kernel, n_col, band),
        out_shape=[jax.ShapeDtypeStruct((halves, n_col, rows_d, LANES), jnp.float32)]
        + [jax.ShapeDtypeStruct((n_row, rows, BX * BY), jnp.bfloat16) for rows in edge_rows],
        in_specs=[smem, smem] + [vmem] * 4,
        out_specs=[vmem] * (1 + len(pieces)),
        scratch_shapes=[pltpu.VMEM((rows, BX * BY), jnp.float32) for rows in edge_rows]
        + [pltpu.VMEM((species, domains, slots), jnp.float32)],
        compiler_params=params,
        name="deposit",
    )(first, send_counts, send_cells, send_species, send_mix, pick)
    dens, sends = made[0], made[1:]
    recvs = [
        lax.ppermute(send, ("row", "col"), [(i, (i + hop) % domains) for i in range(domains)])
        for send, (hop, _, _, _) in zip(sends, pieces)
    ]
    return pl.pallas_call(
        functools.partial(force_kernel, n_col, band),
        out_shape=jax.ShapeDtypeStruct((1, 3, domains, slots), jnp.float32),
        in_specs=[smem, smem] + [vmem] * (9 + len(pieces)),
        out_specs=vmem,
        scratch_shapes=[
            pltpu.VMEM((species, domains, slots), jnp.float32),
            pltpu.VMEM((halves, n_col, rows_v, LANES), jnp.float32),
            pltpu.VMEM((halves, n_col, rows_v, LANES), jnp.float32),
            pltpu.VMEM((halves, n_col, 2 * rows_d, LANES), jnp.float32),
            pltpu.VMEM((4 * rows_d, along_z.shape[1]), jnp.bfloat16),
        ],
        compiler_params=params,
        name="force",
    )(first, send_counts, send_cells, send_species, send_mix, chi, left, right, along_z, off_diag, dens, *recvs)


def solution(mesh):
    spec = P(("row", "col"))
    return jax.shard_map(
        functools.partial(body, mesh.shape["row"], mesh.shape["col"]),
        mesh=mesh,
        in_specs=(spec, spec, spec, spec, P()),
        out_specs=spec,
        check_vma=False,
    )
```

```python
import functools

import jax
import jax.numpy as jnp
import numpy as np
from jax import lax
from jax.experimental import pallas as pl
from jax.experimental.pallas import tpu as pltpu
from jax.sharding import PartitionSpec as P

BX = 16
BY = 16
NZ = 256
LANES = 128
HALF = LANES // BY
REACH = 3

raw_taps = (0.1353352832366127, 0.6065306597126334, 1.0, 0.6065306597126334, 0.1353352832366127)
tap_total = sum(raw_taps)
taps = tuple(t / tap_total for t in raw_taps)
rho_ref = 2.0
inv_kappa = 1.0


def pieces_of(band):
    out = []
    hop, left = 1, REACH
    while left > 0:
        n = min(band, left)
        out.append((hop, band - n, n, -(hop - 1) * band - n))
        out.append((-hop, 0, n, hop * band))
        left -= n
        hop += 1
    return out


def constants_of(species, band):
    pieces = pieces_of(band)
    rows_d = species * band
    rows_h = -(-2 * REACH * species // 8) * 8
    source = [(k, z) for k in range(species) for z in range(band)]
    source += [(k, at + p) for _, _, n, at in pieces for k in range(species) for p in range(n)]
    rows_m = -(-(rows_d + rows_h) // 16) * 16
    left = np.zeros((2 * rows_d, species), np.float32)
    right = np.zeros((species, rows_m), np.float32)
    along_z = np.zeros((2, 2 * rows_d, rows_m), np.float32)
    tap = lambda t: taps[t + 2] if -2 <= t <= 2 else 0.0
    for kind in range(2):
        for k in range(species):
            for z in range(band):
                i = kind * rows_d + k * band + z
                left[i, k] = 1.0
                for j, (l, at) in enumerate(source):
                    right[l, j] = 1.0
                    value = tap(at - z) if kind == 0 else tap(at - z - 1) - tap(at - z + 1)
                    along_z[0, i, j] = -0.5 * value * (0.5 / rho_ref) * float(k != l)
                    along_z[1, i, j] = -0.5 * value * (inv_kappa / rho_ref)
    return left, right, along_z


def exact(a, b, dims=(((1,), (0,)), ((), ()))):
    return lax.dot_general(a, b, dims, precision=lax.Precision.HIGHEST, preferred_element_type=jnp.float32)


def fill_weights(species_ref, mix_ref, wts):
    for k in range(wts.shape[0]):
        onehot = (species_ref[0] == k).astype(jnp.float32)
        wts[k] = (onehot + mix_ref[0, k].astype(jnp.float32)).astype(jnp.bfloat16).astype(jnp.float32)


def banded_of(cells, count, wts, d, first_z, band):
    slots = cells.shape[1]
    z = (cells & (NZ - 1)) - first_z
    z = jnp.where(lax.broadcasted_iota(jnp.int32, (1, slots), 1) < count, z, -1)
    hit = z == lax.broadcasted_iota(jnp.int32, (band, slots), 0)
    parts = [jnp.where(hit, wts[k, pl.ds(d, 1), :], 0.0) for k in range(wts.shape[0])]
    return jnp.concatenate(parts, axis=0)


def table_of(cells):
    plane = lax.shift_right_logical(cells, NZ.bit_length() - 1)
    ids = lax.broadcasted_iota(jnp.int32, (BX * BY, cells.shape[1]), 0)
    return jnp.where(plane == ids, 1.0, 0.0).astype(jnp.bfloat16)


def chunks_of(rows):
    return [(at, min(8, rows - at)) for at in range(0, rows, 8)]


def lane_of(rows):
    return lax.broadcasted_iota(jnp.int32, (rows, LANES), 1)


def lane_x_of(rows):
    return lax.shift_right_logical(lane_of(rows), BY.bit_length() - 1)


def lane_y_of(rows):
    return lane_of(rows) & (BY - 1)


def roll(value, shift):
    return pltpu.roll(value, shift % LANES, 1)


def moved_y(ahead, here, lane_y, t):
    if t > 0:
        return roll(jnp.where(lane_y < t, ahead, here), -t)
    return roll(jnp.where(lane_y >= BY + t, ahead, here), -t)


def moved_x(ahead, here, lane_x, t):
    if t > 0:
        return roll(jnp.where(lane_x < t, ahead, here), -t * BY)
    return roll(jnp.where(lane_x >= HALF + t, ahead, here), -t * BY)


def smoothed(moved, before, here, after, lane):
    one = moved(after, here, lane, 1) + moved(before, here, lane, -1)
    two = moved(after, here, lane, 2) + moved(before, here, lane, -2)
    return taps[2] * here + taps[3] * one + taps[4] * two


def smooth_y(src, dst, h, n_col):
    for at, size in chunks_of(src.shape[2]):
        lane_y = lane_y_of(size)
        rows = [src[h, q, at:at + size] for q in range(n_col)]
        for q in range(n_col):
            before, after = roll(rows[q - 1], -BY), roll(rows[(q + 1) % n_col], BY)
            dst[h, q, at:at + size] = smoothed(moved_y, before, rows[q], after, lane_y)


def smooth_x(src, r, q):
    halves = src.shape[0]
    out = ([], [])
    for at, size in chunks_of(src.shape[2]):
        lane_x = lane_x_of(size)
        a, b = src[(2 * r + halves - 1) % halves, q, at:at + size], src[2 * r, q, at:at + size]
        c, d = src[2 * r + 1, q, at:at + size], src[(2 * r + 2) % halves, q, at:at + size]
        out[0].append(smoothed(moved_x, a, b, c, lane_x))
        out[1].append(smoothed(moved_x, b, c, d, lane_x))
    return out


def membrane_kernel(n_row, n_col, band, counts_ref, cells_hbm, species_hbm, mix_hbm, chi_hbm, left_hbm, right_hbm,
                    along_hbm, out_ref, *refs):
    pieces = pieces_of(band)
    held, refs = refs[:7], refs[7:]
    sends, refs = refs[:len(pieces)], refs[len(pieces):]
    recvs, refs = refs[:len(pieces)], refs[len(pieces):]
    stages, refs = refs[:len(pieces)], refs[len(pieces):]
    wts, raw, turned, edge_raw, edge_turned, fields, maps, load_sem, send_sem, recv_sem = refs
    cells_ref, species_ref, mix_ref, chi_ref, left_ref, right_ref, along_ref = held
    count = wts.shape[0]
    rows_d, rows_h = count * band, edge_raw.shape[2]
    halves, rows_m = 2 * n_row, maps.shape[1]
    bricks = n_row * n_col
    me = lax.axis_index("row") * n_col + lax.axis_index("col")
    first_z = me * band

    loads = [
        pltpu.make_async_copy(src, dst, load_sem.at[i])
        for i, (src, dst) in enumerate(
            zip((cells_hbm, species_hbm, mix_hbm, chi_hbm, left_hbm, right_hbm, along_hbm), held)
        )
    ]
    for load in loads:
        load.start()

    def device_at(hop):
        there = (me + hop + bricks) % bricks
        return (there // n_col, there % n_col)

    barrier = pltpu.get_barrier_semaphore()
    for hop, _, _, _ in pieces:
        pl.semaphore_signal(barrier, inc=1, device_id=device_at(hop), device_id_type=pl.DeviceIdType.MESH)

    def transfer(i, r):
        return pltpu.make_async_remote_copy(
            src_ref=sends[i].at[r],
            dst_ref=recvs[i].at[r],
            send_sem=send_sem.at[i, r],
            recv_sem=recv_sem.at[i, r],
            device_id=device_at(pieces[i][0]),
            device_id_type=pl.DeviceIdType.MESH,
        )

    for load in loads[:3]:
        load.wait()
    fill_weights(species_ref, mix_ref, wts)
    used = 2 * REACH * count
    if rows_h > used:
        edge_raw[:, :, used:] = jnp.zeros((halves, n_col, rows_h - used, LANES), jnp.float32)
    pl.semaphore_wait(barrier, len(pieces))

    def deposit(r, carry):
        for q in range(n_col):
            d = r * n_col + q
            cells = cells_ref[0, pl.ds(d, 1), :]
            banded = banded_of(cells, counts_ref[0, d], wts, d, first_z, band)
            tile = lax.dot_general(
                banded.astype(jnp.bfloat16), table_of(cells), (((1,), (1,)), ((), ())),
                preferred_element_type=jnp.float32,
            )
            raw[2 * r, q] = tile[:, :LANES]
            raw[2 * r + 1, q] = tile[:, LANES:]
            for stage, (_, first, n, _) in zip(stages, pieces):
                for k in range(count):
                    to = (q * count + k) * n
                    stage[to:to + n, :] = tile[k * band + first:k * band + first + n]
        for i in range(len(pieces)):
            sends[i][r] = stages[i][...].astype(jnp.bfloat16)
            transfer(i, r).start()
        return carry

    lax.fori_loop(0, n_row, deposit, 0)

    for load in loads[3:]:
        load.wait()
    chi = chi_ref[...]
    mixing = exact(exact(left_ref[...], chi), right_ref[...])
    mixing += exact(exact(left_ref[...], chi, (((1,), (1,)), ((), ()))), right_ref[...])
    full = mixing * along_ref[0] + along_ref[1]
    high = full.astype(jnp.bfloat16)
    maps[:2 * rows_d] = high
    maps[2 * rows_d:] = (full - high.astype(jnp.float32)).astype(jnp.bfloat16)

    def inner_y(h, carry):
        smooth_y(raw, turned, h, n_col)
        return carry

    lax.fori_loop(0, halves, inner_y, 0)

    def inner_x(d, carry):
        r, q = d // n_col, d % n_col
        for h, done in enumerate(smooth_x(turned, r, q)):
            for (at, size), value in zip(chunks_of(rows_d), done):
                raw[2 * r + h, q, at:at + size] = value
        return carry

    lax.fori_loop(0, bricks, inner_x, 0, unroll=2)

    def edge_y(r, carry):
        for i in range(len(pieces)):
            transfer(i, r).wait_recv()
        got = [recv[r].astype(jnp.float32) for recv in recvs]
        for q in range(n_col):
            at = 0
            for part, (_, _, n, _) in zip(got, pieces):
                rows = n * count
                for h in range(2):
                    edge_raw[2 * r + h, q, at:at + rows] = part[q * rows:(q + 1) * rows, h * LANES:(h + 1) * LANES]
                at += rows
        for h in range(2):
            smooth_y(edge_raw, edge_turned, 2 * r + h, n_col)
        return carry

    lax.fori_loop(0, n_row, edge_y, 0)

    def to_fields(d, carry):
        r, q = d // n_col, d % n_col
        done = []
        for h, edges in enumerate(smooth_x(edge_turned, r, q)):
            parts = [raw[2 * r + h, q]] + edges
            if rows_m > rows_d + rows_h:
                parts.append(jnp.zeros((rows_m - rows_d - rows_h, LANES), jnp.float32))
            done.append(jnp.concatenate(parts, axis=0))
        value = jnp.concatenate(done, axis=1)
        top = value.astype(jnp.bfloat16)
        rest = (value - top.astype(jnp.float32)).astype(jnp.bfloat16)
        first = jnp.dot(maps[...], top, preferred_element_type=jnp.float32)
        field = first[:2 * rows_d] + first[2 * rows_d:]
        field = field + jnp.dot(maps[:2 * rows_d], rest, preferred_element_type=jnp.float32)
        fields[2 * r, q] = field[:, :LANES]
        fields[2 * r + 1, q] = field[:, LANES:]
        return carry

    lax.fori_loop(0, bricks, to_fields, 0, unroll=2)

    def gather(d, carry):
        r, q = d // n_col, d % n_col
        grads = ([], [], [])
        for at, size in chunks_of(rows_d):
            lane_x, lane_y = lane_x_of(size), lane_y_of(size)
            sides = ([], [])
            for h in range(2):
                half = 2 * r + h
                here = fields[half, q, at:at + size]
                back, on = (fields[(half + step + halves) % halves, q, at:at + size] for step in (-1, 1))
                sides[0].append(moved_x(on, here, lane_x, 1) - moved_x(back, here, lane_x, -1))
                back, on = (fields[half, (q + step + n_col) % n_col, at:at + size] for step in (-1, 1))
                back, on = roll(back, -BY), roll(on, BY)
                sides[1].append(moved_y(on, here, lane_y, 1) - moved_y(back, here, lane_y, -1))
            for a in range(2):
                grads[a].append(jnp.concatenate(sides[a], axis=1))
        grads[2].append(
            jnp.concatenate([fields[2 * r, q, rows_d:], fields[2 * r + 1, q, rows_d:]], axis=1)
        )
        grad = jnp.concatenate(grads[0] + grads[1] + grads[2], axis=0)
        cells = cells_ref[0, pl.ds(d, 1), :]
        banded = banded_of(cells, counts_ref[0, d], wts, d, first_z, band)
        top = grad.astype(jnp.bfloat16)
        rest = (grad - top.astype(jnp.float32)).astype(jnp.bfloat16)
        value = jnp.dot(
            jnp.concatenate([top, rest], axis=0), table_of(cells), preferred_element_type=jnp.float32
        )
        for a in range(3):
            low, high = a * rows_d, (a + 1) * rows_d
            value_a = value[low:high] + value[3 * rows_d + low:3 * rows_d + high]
            out_ref[0, a, pl.ds(d, 1), :] = jnp.sum(value_a * banded, axis=0, keepdims=True)
        return carry

    lax.fori_loop(0, bricks, gather, 0, unroll=2)

    def finish(r, carry):
        for i in range(len(pieces)):
            transfer(i, r).wait_send()
        return carry

    lax.fori_loop(0, n_row, finish, 0)


def body(n_row, n_col, send_cells, send_species, send_mix, send_counts, chi):
    species, domains, slots = send_mix.shape[1:]
    band = NZ // domains
    halves = 2 * n_row
    rows_d = species * band
    pieces = pieces_of(band)
    left, right, along_z = constants_of(species, band)
    rows_h = -(-2 * REACH * species // 8) * 8
    edge_rows = [n_col * n * species for _, _, n, _ in pieces]
    operands = (send_cells, send_species, send_mix, chi, left, right, along_z)
    grid = lambda rows: pltpu.VMEM((halves, n_col, rows, LANES), jnp.float32)
    return pl.pallas_call(
        functools.partial(membrane_kernel, n_row, n_col, band),
        out_shape=jax.ShapeDtypeStruct((1, 3, domains, slots), jnp.float32),
        in_specs=[pl.BlockSpec(memory_space=pltpu.SMEM)] + [pl.BlockSpec(memory_space=pl.ANY)] * 7,
        out_specs=pl.BlockSpec(memory_space=pltpu.VMEM),
        scratch_shapes=[pltpu.VMEM(operand.shape, operand.dtype) for operand in operands]
        + [pltpu.VMEM((n_row, rows, BX * BY), jnp.bfloat16) for rows in edge_rows] * 2
        + [pltpu.VMEM((rows, BX * BY), jnp.float32) for rows in edge_rows]
        + [pltpu.VMEM((species, domains, slots), jnp.float32)]
        + [grid(rows_d), grid(rows_d), grid(rows_h), grid(rows_h), grid(2 * rows_d)]
        + [pltpu.VMEM((4 * rows_d, along_z.shape[2]), jnp.bfloat16)]
        + [
            pltpu.SemaphoreType.DMA((7,)),
            pltpu.SemaphoreType.DMA((len(pieces), n_row)),
            pltpu.SemaphoreType.DMA((len(pieces), n_row)),
        ],
        compiler_params=pltpu.CompilerParams(
            collective_id=0, has_side_effects=True, vmem_limit_bytes=56 * 2**20
        ),
        name="membrane",
    )(send_counts, *operands)


def solution(mesh):
    spec = P(("row", "col"))
    return jax.shard_map(
        functools.partial(body, mesh.shape["row"], mesh.shape["col"]),
        mesh=mesh,
        in_specs=(spec, spec, spec, spec, P()),
        out_specs=spec,
        check_vma=False,
    )
```

```python
import functools

import jax
import jax.numpy as jnp
import numpy as np
from jax import lax
from jax.experimental import pallas as pl
from jax.experimental.pallas import tpu as pltpu
from jax.sharding import PartitionSpec as P

BX = 16
BY = 16
NZ = 256
LANES = 128
HALF = LANES // BY
REACH = 3

raw_taps = (0.1353352832366127, 0.6065306597126334, 1.0, 0.6065306597126334, 0.1353352832366127)
tap_total = sum(raw_taps)
taps = tuple(t / tap_total for t in raw_taps)
rho_ref = 2.0
inv_kappa = 1.0


def pieces_of(band):
    out = []
    hop, left = 1, REACH
    while left > 0:
        n = min(band, left)
        out.append((hop, band - n, n, -(hop - 1) * band - n))
        out.append((-hop, 0, n, hop * band))
        left -= n
        hop += 1
    return out


def constants_of(species, band):
    pieces = pieces_of(band)
    rows_d = species * band
    rows_h = -(-2 * REACH * species // 8) * 8
    source = [(k, z) for k in range(species) for z in range(band)]
    source += [(k, at + p) for _, _, n, at in pieces for k in range(species) for p in range(n)]
    rows_m = -(-(rows_d + rows_h) // 16) * 16
    left = np.zeros((2 * rows_d, species), np.float32)
    right = np.zeros((species, rows_m), np.float32)
    along_z = np.zeros((2, 2 * rows_d, rows_m), np.float32)
    tap = lambda t: taps[t + 2] if -2 <= t <= 2 else 0.0
    for kind in range(2):
        for k in range(species):
            for z in range(band):
                i = kind * rows_d + k * band + z
                left[i, k] = 1.0
                for j, (l, at) in enumerate(source):
                    right[l, j] = 1.0
                    value = tap(at - z) if kind == 0 else tap(at - z - 1) - tap(at - z + 1)
                    along_z[0, i, j] = -0.5 * value * (0.5 / rho_ref) * float(k != l)
                    along_z[1, i, j] = -0.5 * value * (inv_kappa / rho_ref)
    return left, right, along_z


def exact(a, b, dims=(((1,), (0,)), ((), ()))):
    return lax.dot_general(a, b, dims, precision=lax.Precision.HIGHEST, preferred_element_type=jnp.float32)


def fill_weights(species_ref, mix_ref, wts):
    for k in range(wts.shape[0]):
        onehot = (species_ref[0] == k).astype(jnp.float32)
        wts[k] = (onehot + mix_ref[0, k].astype(jnp.float32)).astype(jnp.bfloat16).astype(jnp.float32)


def banded_of(cells, count, wts, d, first_z, band):
    slots = cells.shape[1]
    z = (cells & (NZ - 1)) - first_z
    z = jnp.where(lax.broadcasted_iota(jnp.int32, (1, slots), 1) < count, z, -1)
    hit = z == lax.broadcasted_iota(jnp.int32, (band, slots), 0)
    parts = [jnp.where(hit, wts[k, pl.ds(d, 1), :], 0.0) for k in range(wts.shape[0])]
    return jnp.concatenate(parts, axis=0)


def table_of(cells):
    plane = lax.shift_right_logical(cells, NZ.bit_length() - 1)
    ids = lax.broadcasted_iota(jnp.int32, (BX * BY, cells.shape[1]), 0)
    return jnp.where(plane == ids, 1.0, 0.0).astype(jnp.bfloat16)


def chunks_of(rows):
    return [(at, min(8, rows - at)) for at in range(0, rows, 8)]


def lane_of(rows):
    return lax.broadcasted_iota(jnp.int32, (rows, LANES), 1)


def lane_x_of(rows):
    return lax.shift_right_logical(lane_of(rows), BY.bit_length() - 1)


def lane_y_of(rows):
    return lane_of(rows) & (BY - 1)


def roll(value, shift):
    return pltpu.roll(value, shift % LANES, 1)


def moved_y(ahead, here, lane_y, t):
    if t > 0:
        return roll(jnp.where(lane_y < t, ahead, here), -t)
    return roll(jnp.where(lane_y >= BY + t, ahead, here), -t)


def moved_x(ahead, here, lane_x, t):
    if t > 0:
        return roll(jnp.where(lane_x < t, ahead, here), -t * BY)
    return roll(jnp.where(lane_x >= HALF + t, ahead, here), -t * BY)


def smoothed(moved, before, here, after, lane):
    one = moved(after, here, lane, 1) + moved(before, here, lane, -1)
    two = moved(after, here, lane, 2) + moved(before, here, lane, -2)
    return taps[2] * here + taps[3] * one + taps[4] * two


def smooth_y(src, r, q):
    n_col = src.shape[1]
    out = ([], [])
    for h in range(2):
        for at, size in chunks_of(src.shape[2]):
            lane_y = lane_y_of(size)
            before = src[2 * r + h, (q + n_col - 1) % n_col, at:at + size]
            after = src[2 * r + h, (q + 1) % n_col, at:at + size]
            here = src[2 * r + h, q, at:at + size]
            out[h].append(smoothed(moved_y, roll(before, -BY), here, roll(after, BY), lane_y))
    return out


def keep(dst, r, q, done):
    for h in range(2):
        for (at, size), value in zip(chunks_of(dst.shape[2]), done[h]):
            dst[2 * r + h, q, at:at + size] = value


def smooth_x(src, r, q):
    halves = src.shape[0]
    out = ([], [])
    for at, size in chunks_of(src.shape[2]):
        lane_x = lane_x_of(size)
        a, b = src[(2 * r + halves - 1) % halves, q, at:at + size], src[2 * r, q, at:at + size]
        c, d = src[2 * r + 1, q, at:at + size], src[(2 * r + 2) % halves, q, at:at + size]
        out[0].append(smoothed(moved_x, a, b, c, lane_x))
        out[1].append(smoothed(moved_x, b, c, d, lane_x))
    return out


def membrane_kernel(n_row, n_col, band, counts_ref, cells_hbm, species_hbm, mix_hbm, chi_hbm, left_hbm, right_hbm,
                    along_hbm, out_ref, *refs):
    pieces = pieces_of(band)
    held, refs = refs[:7], refs[7:]
    sends, refs = refs[:len(pieces)], refs[len(pieces):]
    recvs, refs = refs[:len(pieces)], refs[len(pieces):]
    stages, refs = refs[:len(pieces)], refs[len(pieces):]
    wts, raw, turned, edge_raw, edge_turned, fields, maps, load_sem, send_sem, recv_sem = refs
    cells_ref, species_ref, mix_ref, chi_ref, left_ref, right_ref, along_ref = held
    count = wts.shape[0]
    rows_d, rows_h = count * band, edge_raw.shape[2]
    halves, rows_m = 2 * n_row, maps.shape[1]
    bricks = n_row * n_col
    me = lax.axis_index("row") * n_col + lax.axis_index("col")
    first_z = me * band

    loads = [
        pltpu.make_async_copy(src, dst, load_sem.at[i])
        for i, (src, dst) in enumerate(
            zip((cells_hbm, species_hbm, mix_hbm, chi_hbm, left_hbm, right_hbm, along_hbm), held)
        )
    ]
    for load in loads:
        load.start()

    def device_at(hop):
        there = (me + hop + bricks) % bricks
        return (there // n_col, there % n_col)

    barrier = pltpu.get_barrier_semaphore()
    for hop, _, _, _ in pieces:
        pl.semaphore_signal(barrier, inc=1, device_id=device_at(hop), device_id_type=pl.DeviceIdType.MESH)

    def transfer(i, r):
        return pltpu.make_async_remote_copy(
            src_ref=sends[i].at[r],
            dst_ref=recvs[i].at[r],
            send_sem=send_sem.at[i, r],
            recv_sem=recv_sem.at[i, r],
            device_id=device_at(pieces[i][0]),
            device_id_type=pl.DeviceIdType.MESH,
        )

    for load in loads[:3]:
        load.wait()
    fill_weights(species_ref, mix_ref, wts)
    used = 2 * REACH * count
    if rows_h > used:
        edge_raw[:, :, used:] = jnp.zeros((halves, n_col, rows_h - used, LANES), jnp.float32)
    pl.semaphore_wait(barrier, len(pieces))

    def deposit(r, carry):
        for q in range(n_col):
            d = r * n_col + q
            cells = cells_ref[0, pl.ds(d, 1), :]
            banded = banded_of(cells, counts_ref[0, d], wts, d, first_z, band)
            tile = lax.dot_general(
                banded.astype(jnp.bfloat16), table_of(cells), (((1,), (1,)), ((), ())),
                preferred_element_type=jnp.float32,
            )
            raw[2 * r, q] = tile[:, :LANES]
            raw[2 * r + 1, q] = tile[:, LANES:]
            for stage, (_, first, n, _) in zip(stages, pieces):
                for k in range(count):
                    to = (q * count + k) * n
                    stage[to:to + n, :] = tile[k * band + first:k * band + first + n]
        for i in range(len(pieces)):
            sends[i][r] = stages[i][...].astype(jnp.bfloat16)
            transfer(i, r).start()
        return carry

    lax.fori_loop(0, n_row, deposit, 0)

    for load in loads[3:]:
        load.wait()
    chi = chi_ref[...]
    mixing = exact(exact(left_ref[...], chi), right_ref[...])
    mixing += exact(exact(left_ref[...], chi, (((1,), (1,)), ((), ()))), right_ref[...])
    full = mixing * along_ref[0] + along_ref[1]
    high = full.astype(jnp.bfloat16)
    maps[:2 * rows_d] = high
    maps[2 * rows_d:] = (full - high.astype(jnp.float32)).astype(jnp.bfloat16)

    def inner_y(d, carry):
        r, q = d // n_col, d % n_col
        keep(turned, r, q, smooth_y(raw, r, q))
        return carry

    lax.fori_loop(0, bricks, inner_y, 0, unroll=2)

    def inner_x(d, carry):
        r, q = d // n_col, d % n_col
        keep(raw, r, q, smooth_x(turned, r, q))
        return carry

    lax.fori_loop(0, bricks, inner_x, 0, unroll=2)

    def edge_y(r, carry):
        for i in range(len(pieces)):
            transfer(i, r).wait_recv()
        got = [recv[r].astype(jnp.float32) for recv in recvs]
        for q in range(n_col):
            at = 0
            for part, (_, _, n, _) in zip(got, pieces):
                rows = n * count
                for h in range(2):
                    edge_raw[2 * r + h, q, at:at + rows] = part[q * rows:(q + 1) * rows, h * LANES:(h + 1) * LANES]
                at += rows

        def one(q, carry):
            keep(edge_turned, r, q, smooth_y(edge_raw, r, q))
            return carry

        return lax.fori_loop(0, n_col, one, carry, unroll=2)

    lax.fori_loop(0, n_row, edge_y, 0)

    def to_fields(d, carry):
        r, q = d // n_col, d % n_col
        done = []
        for h, edges in enumerate(smooth_x(edge_turned, r, q)):
            parts = [raw[2 * r + h, q]] + edges
            if rows_m > rows_d + rows_h:
                parts.append(jnp.zeros((rows_m - rows_d - rows_h, LANES), jnp.float32))
            done.append(jnp.concatenate(parts, axis=0))
        value = jnp.concatenate(done, axis=1)
        top = value.astype(jnp.bfloat16)
        rest = (value - top.astype(jnp.float32)).astype(jnp.bfloat16)
        first = jnp.dot(maps[...], top, preferred_element_type=jnp.float32)
        field = first[:2 * rows_d] + first[2 * rows_d:]
        field = field + jnp.dot(maps[:2 * rows_d], rest, preferred_element_type=jnp.float32)
        fields[2 * r, q] = field[:, :LANES]
        fields[2 * r + 1, q] = field[:, LANES:]
        return carry

    lax.fori_loop(0, bricks, to_fields, 0, unroll=2)

    def gather(d, carry):
        r, q = d // n_col, d % n_col
        grads = ([], [], [])
        for at, size in chunks_of(rows_d):
            lane_x, lane_y = lane_x_of(size), lane_y_of(size)
            sides = ([], [])
            for h in range(2):
                half = 2 * r + h
                here = fields[half, q, at:at + size]
                back, on = (fields[(half + step + halves) % halves, q, at:at + size] for step in (-1, 1))
                sides[0].append(moved_x(on, here, lane_x, 1) - moved_x(back, here, lane_x, -1))
                back, on = (fields[half, (q + step + n_col) % n_col, at:at + size] for step in (-1, 1))
                back, on = roll(back, -BY), roll(on, BY)
                sides[1].append(moved_y(on, here, lane_y, 1) - moved_y(back, here, lane_y, -1))
            for a in range(2):
                grads[a].append(jnp.concatenate(sides[a], axis=1))
        grads[2].append(
            jnp.concatenate([fields[2 * r, q, rows_d:], fields[2 * r + 1, q, rows_d:]], axis=1)
        )
        grad = jnp.concatenate(grads[0] + grads[1] + grads[2], axis=0)
        cells = cells_ref[0, pl.ds(d, 1), :]
        banded = banded_of(cells, counts_ref[0, d], wts, d, first_z, band)
        top = grad.astype(jnp.bfloat16)
        rest = (grad - top.astype(jnp.float32)).astype(jnp.bfloat16)
        value = jnp.dot(
            jnp.concatenate([top, rest], axis=0), table_of(cells), preferred_element_type=jnp.float32
        )
        for a in range(3):
            low, high = a * rows_d, (a + 1) * rows_d
            value_a = value[low:high] + value[3 * rows_d + low:3 * rows_d + high]
            out_ref[0, a, pl.ds(d, 1), :] = jnp.sum(value_a * banded, axis=0, keepdims=True)
        return carry

    lax.fori_loop(0, bricks, gather, 0, unroll=2)

    def finish(r, carry):
        for i in range(len(pieces)):
            transfer(i, r).wait_send()
        return carry

    lax.fori_loop(0, n_row, finish, 0)


def body(n_row, n_col, send_cells, send_species, send_mix, send_counts, chi):
    species, domains, slots = send_mix.shape[1:]
    band = NZ // domains
    halves = 2 * n_row
    rows_d = species * band
    pieces = pieces_of(band)
    left, right, along_z = constants_of(species, band)
    rows_h = -(-2 * REACH * species // 8) * 8
    edge_rows = [n_col * n * species for _, _, n, _ in pieces]
    operands = (send_cells, send_species, send_mix, chi, left, right, along_z)
    grid = lambda rows: pltpu.VMEM((halves, n_col, rows, LANES), jnp.float32)
    return pl.pallas_call(
        functools.partial(membrane_kernel, n_row, n_col, band),
        out_shape=jax.ShapeDtypeStruct((1, 3, domains, slots), jnp.float32),
        in_specs=[pl.BlockSpec(memory_space=pltpu.SMEM)] + [pl.BlockSpec(memory_space=pl.ANY)] * 7,
        out_specs=pl.BlockSpec(memory_space=pltpu.VMEM),
        scratch_shapes=[pltpu.VMEM(operand.shape, operand.dtype) for operand in operands]
        + [pltpu.VMEM((n_row, rows, BX * BY), jnp.bfloat16) for rows in edge_rows] * 2
        + [pltpu.VMEM((rows, BX * BY), jnp.float32) for rows in edge_rows]
        + [pltpu.VMEM((species, domains, slots), jnp.float32)]
        + [grid(rows_d), grid(rows_d), grid(rows_h), grid(rows_h), grid(2 * rows_d)]
        + [pltpu.VMEM((4 * rows_d, along_z.shape[2]), jnp.bfloat16)]
        + [
            pltpu.SemaphoreType.DMA((7,)),
            pltpu.SemaphoreType.DMA((len(pieces), n_row)),
            pltpu.SemaphoreType.DMA((len(pieces), n_row)),
        ],
        compiler_params=pltpu.CompilerParams(
            collective_id=0, has_side_effects=True, vmem_limit_bytes=56 * 2**20
        ),
        name="membrane",
    )(send_counts, *operands)


def solution(mesh):
    spec = P(("row", "col"))
    return jax.shard_map(
        functools.partial(body, mesh.shape["row"], mesh.shape["col"]),
        mesh=mesh,
        in_specs=(spec, spec, spec, spec, P()),
        out_specs=spec,
        check_vma=False,
    )
```

```python
import functools

import jax
import jax.numpy as jnp
import numpy as np
from jax import lax
from jax.experimental import pallas as pl
from jax.experimental.pallas import tpu as pltpu
from jax.sharding import PartitionSpec as P

BX = 16
BY = 16
NZ = 256
LANES = 128
HALF = LANES // BY
REACH = 3

raw_taps = (0.1353352832366127, 0.6065306597126334, 1.0, 0.6065306597126334, 0.1353352832366127)
tap_total = sum(raw_taps)
taps = tuple(t / tap_total for t in raw_taps)
rho_ref = 2.0
inv_kappa = 1.0


def pieces_of(band):
    out = []
    hop, left = 1, REACH
    while left > 0:
        n = min(band, left)
        out.append((hop, band - n, n, -(hop - 1) * band - n))
        out.append((-hop, 0, n, hop * band))
        left -= n
        hop += 1
    return out


def constants_of(species, band):
    pieces = pieces_of(band)
    rows_d = species * band
    rows_h = -(-2 * REACH * species // 8) * 8
    source = [(k, z) for k in range(species) for z in range(band)]
    source += [(k, at + p) for _, _, n, at in pieces for k in range(species) for p in range(n)]
    rows_m = -(-(rows_d + rows_h) // 16) * 16
    left = np.zeros((2 * rows_d, species), np.float32)
    right = np.zeros((species, rows_m), np.float32)
    along_z = np.zeros((2, 2 * rows_d, rows_m), np.float32)
    tap = lambda t: taps[t + 2] if -2 <= t <= 2 else 0.0
    for kind in range(2):
        for k in range(species):
            for z in range(band):
                i = kind * rows_d + k * band + z
                left[i, k] = 1.0
                for j, (l, at) in enumerate(source):
                    right[l, j] = 1.0
                    value = tap(at - z) if kind == 0 else tap(at - z - 1) - tap(at - z + 1)
                    along_z[0, i, j] = -0.5 * value * (0.5 / rho_ref) * float(k != l)
                    along_z[1, i, j] = -0.5 * value * (inv_kappa / rho_ref)
    return left, right, along_z


def exact(a, b, dims=(((1,), (0,)), ((), ()))):
    return lax.dot_general(a, b, dims, precision=lax.Precision.HIGHEST, preferred_element_type=jnp.float32)


def fill_weights(species_ref, mix_ref, wts):
    for k in range(wts.shape[0]):
        onehot = (species_ref[0] == k).astype(jnp.float32)
        wts[k] = (onehot + mix_ref[0, k].astype(jnp.float32)).astype(jnp.bfloat16).astype(jnp.float32)


def banded_of(cells, count, wts, d, first_z, band):
    slots = cells.shape[1]
    z = (cells & (NZ - 1)) - first_z
    z = jnp.where(lax.broadcasted_iota(jnp.int32, (1, slots), 1) < count, z, -1)
    hit = z == lax.broadcasted_iota(jnp.int32, (band, slots), 0)
    parts = [jnp.where(hit, wts[k, pl.ds(d, 1), :], 0.0) for k in range(wts.shape[0])]
    return jnp.concatenate(parts, axis=0)


def table_of(cells, ids):
    plane = lax.shift_right_logical(cells, NZ.bit_length() - 1).astype(jnp.float32).astype(jnp.bfloat16)
    one, none = jnp.ones((), jnp.bfloat16), jnp.zeros((), jnp.bfloat16)
    numbers = ids[...]
    parts = [
        jnp.where(plane[:, at:at + LANES] == numbers, one, none) for at in range(0, cells.shape[1], LANES)
    ]
    return jnp.concatenate(parts, axis=1)


def chunks_of(rows):
    return [(at, min(8, rows - at)) for at in range(0, rows, 8)]


def lane_of(rows):
    return lax.broadcasted_iota(jnp.int32, (rows, LANES), 1)


def lane_x_of(rows):
    return lax.shift_right_logical(lane_of(rows), BY.bit_length() - 1)


def lane_y_of(rows):
    return lane_of(rows) & (BY - 1)


def roll(value, shift):
    return pltpu.roll(value, shift % LANES, 1)


def moved_y(ahead, here, lane_y, t):
    if t > 0:
        return roll(jnp.where(lane_y < t, ahead, here), -t)
    return roll(jnp.where(lane_y >= BY + t, ahead, here), -t)


def moved_x(ahead, here, lane_x, t):
    if t > 0:
        return roll(jnp.where(lane_x < t, ahead, here), -t * BY)
    return roll(jnp.where(lane_x >= HALF + t, ahead, here), -t * BY)


def smoothed(moved, before, here, after, lane):
    one = moved(after, here, lane, 1) + moved(before, here, lane, -1)
    two = moved(after, here, lane, 2) + moved(before, here, lane, -2)
    return taps[2] * here + taps[3] * one + taps[4] * two


def smooth_y(src, r, q):
    n_col = src.shape[1]
    out = ([], [])
    for h in range(2):
        for at, size in chunks_of(src.shape[2]):
            lane_y = lane_y_of(size)
            before = src[2 * r + h, (q + n_col - 1) % n_col, at:at + size]
            after = src[2 * r + h, (q + 1) % n_col, at:at + size]
            here = src[2 * r + h, q, at:at + size]
            out[h].append(smoothed(moved_y, roll(before, -BY), here, roll(after, BY), lane_y))
    return out


def keep(dst, r, q, done):
    for h in range(2):
        for (at, size), value in zip(chunks_of(dst.shape[2]), done[h]):
            dst[2 * r + h, q, at:at + size] = value


def smooth_x(src, r, q):
    halves = src.shape[0]
    out = ([], [])
    for at, size in chunks_of(src.shape[2]):
        lane_x = lane_x_of(size)
        a, b = src[(2 * r + halves - 1) % halves, q, at:at + size], src[2 * r, q, at:at + size]
        c, d = src[2 * r + 1, q, at:at + size], src[(2 * r + 2) % halves, q, at:at + size]
        out[0].append(smoothed(moved_x, a, b, c, lane_x))
        out[1].append(smoothed(moved_x, b, c, d, lane_x))
    return out


def membrane_kernel(n_row, n_col, band, counts_ref, cells_hbm, species_hbm, mix_hbm, chi_hbm, left_hbm, right_hbm,
                    along_hbm, out_ref, *refs):
    pieces = pieces_of(band)
    held, refs = refs[:7], refs[7:]
    sends, refs = refs[:len(pieces)], refs[len(pieces):]
    recvs, refs = refs[:len(pieces)], refs[len(pieces):]
    stages, refs = refs[:len(pieces)], refs[len(pieces):]
    wts, raw, turned, edge_raw, edge_turned, fields, maps, ids, load_sem, send_sem, recv_sem = refs
    cells_ref, species_ref, mix_ref, chi_ref, left_ref, right_ref, along_ref = held
    count = wts.shape[0]
    rows_d, rows_h = count * band, edge_raw.shape[2]
    halves, rows_m = 2 * n_row, maps.shape[1]
    bricks = n_row * n_col
    me = lax.axis_index("row") * n_col + lax.axis_index("col")
    first_z = me * band

    loads = [
        pltpu.make_async_copy(src, dst, load_sem.at[i])
        for i, (src, dst) in enumerate(
            zip((cells_hbm, species_hbm, mix_hbm, chi_hbm, left_hbm, right_hbm, along_hbm), held)
        )
    ]
    for load in loads:
        load.start()

    def device_at(hop):
        there = (me + hop + bricks) % bricks
        return (there // n_col, there % n_col)

    barrier = pltpu.get_barrier_semaphore()
    for hop, _, _, _ in pieces:
        pl.semaphore_signal(barrier, inc=1, device_id=device_at(hop), device_id_type=pl.DeviceIdType.MESH)

    def transfer(i, r):
        return pltpu.make_async_remote_copy(
            src_ref=sends[i].at[r],
            dst_ref=recvs[i].at[r],
            send_sem=send_sem.at[i, r],
            recv_sem=recv_sem.at[i, r],
            device_id=device_at(pieces[i][0]),
            device_id_type=pl.DeviceIdType.MESH,
        )

    for load in loads[:3]:
        load.wait()
    fill_weights(species_ref, mix_ref, wts)
    ids[...] = lax.broadcasted_iota(jnp.int32, ids.shape, 0).astype(jnp.float32).astype(jnp.bfloat16)
    used = 2 * REACH * count
    if rows_h > used:
        edge_raw[:, :, used:] = jnp.zeros((halves, n_col, rows_h - used, LANES), jnp.float32)
    pl.semaphore_wait(barrier, len(pieces))

    def deposit(r, carry):
        for q in range(n_col):
            d = r * n_col + q
            cells = cells_ref[0, pl.ds(d, 1), :]
            banded = banded_of(cells, counts_ref[0, d], wts, d, first_z, band)
            tile = lax.dot_general(
                banded.astype(jnp.bfloat16), table_of(cells, ids), (((1,), (1,)), ((), ())),
                preferred_element_type=jnp.float32,
            )
            raw[2 * r, q] = tile[:, :LANES]
            raw[2 * r + 1, q] = tile[:, LANES:]
            for stage, (_, first, n, _) in zip(stages, pieces):
                for k in range(count):
                    to = (q * count + k) * n
                    stage[to:to + n, :] = tile[k * band + first:k * band + first + n]
        for i in range(len(pieces)):
            sends[i][r] = stages[i][...].astype(jnp.bfloat16)
            transfer(i, r).start()
        return carry

    lax.fori_loop(0, n_row, deposit, 0)

    for load in loads[3:]:
        load.wait()
    chi = chi_ref[...]
    mixing = exact(exact(left_ref[...], chi), right_ref[...])
    mixing += exact(exact(left_ref[...], chi, (((1,), (1,)), ((), ()))), right_ref[...])
    full = mixing * along_ref[0] + along_ref[1]
    high = full.astype(jnp.bfloat16)
    maps[:2 * rows_d] = high
    maps[2 * rows_d:] = (full - high.astype(jnp.float32)).astype(jnp.bfloat16)

    def inner_y(d, carry):
        r, q = d // n_col, d % n_col
        keep(turned, r, q, smooth_y(raw, r, q))
        return carry

    lax.fori_loop(0, bricks, inner_y, 0, unroll=2)

    def inner_x(d, carry):
        r, q = d // n_col, d % n_col
        keep(raw, r, q, smooth_x(turned, r, q))
        return carry

    lax.fori_loop(0, bricks, inner_x, 0, unroll=4)

    def edge_y(r, carry):
        for i in range(len(pieces)):
            transfer(i, r).wait_recv()
        got = [recv[r].astype(jnp.float32) for recv in recvs]
        for q in range(n_col):
            at = 0
            for part, (_, _, n, _) in zip(got, pieces):
                rows = n * count
                for h in range(2):
                    edge_raw[2 * r + h, q, at:at + rows] = part[q * rows:(q + 1) * rows, h * LANES:(h + 1) * LANES]
                at += rows

        def one(q, carry):
            keep(edge_turned, r, q, smooth_y(edge_raw, r, q))
            return carry

        return lax.fori_loop(0, n_col, one, carry, unroll=2)

    lax.fori_loop(0, n_row, edge_y, 0)

    def to_fields(d, carry):
        r, q = d // n_col, d % n_col
        done = []
        for h, edges in enumerate(smooth_x(edge_turned, r, q)):
            parts = [raw[2 * r + h, q]] + edges
            if rows_m > rows_d + rows_h:
                parts.append(jnp.zeros((rows_m - rows_d - rows_h, LANES), jnp.float32))
            done.append(jnp.concatenate(parts, axis=0))
        value = jnp.concatenate(done, axis=1)
        top = value.astype(jnp.bfloat16)
        rest = (value - top.astype(jnp.float32)).astype(jnp.bfloat16)
        first = jnp.dot(maps[...], top, preferred_element_type=jnp.float32)
        field = first[:2 * rows_d] + first[2 * rows_d:]
        field = field + jnp.dot(maps[:2 * rows_d], rest, preferred_element_type=jnp.float32)
        fields[2 * r, q] = field[:, :LANES]
        fields[2 * r + 1, q] = field[:, LANES:]
        return carry

    lax.fori_loop(0, bricks, to_fields, 0, unroll=4)

    def gather(d, carry):
        r, q = d // n_col, d % n_col
        grads = ([], [], [])
        for at, size in chunks_of(rows_d):
            lane_x, lane_y = lane_x_of(size), lane_y_of(size)
            sides = ([], [])
            for h in range(2):
                half = 2 * r + h
                here = fields[half, q, at:at + size]
                back, on = (fields[(half + step + halves) % halves, q, at:at + size] for step in (-1, 1))
                sides[0].append(moved_x(on, here, lane_x, 1) - moved_x(back, here, lane_x, -1))
                back, on = (fields[half, (q + step + n_col) % n_col, at:at + size] for step in (-1, 1))
                back, on = roll(back, -BY), roll(on, BY)
                sides[1].append(moved_y(on, here, lane_y, 1) - moved_y(back, here, lane_y, -1))
            for a in range(2):
                grads[a].append(jnp.concatenate(sides[a], axis=1))
        grads[2].append(
            jnp.concatenate([fields[2 * r, q, rows_d:], fields[2 * r + 1, q, rows_d:]], axis=1)
        )
        grad = jnp.concatenate(grads[0] + grads[1] + grads[2], axis=0)
        cells = cells_ref[0, pl.ds(d, 1), :]
        banded = banded_of(cells, counts_ref[0, d], wts, d, first_z, band)
        top = grad.astype(jnp.bfloat16)
        rest = (grad - top.astype(jnp.float32)).astype(jnp.bfloat16)
        value = jnp.dot(
            jnp.concatenate([top, rest], axis=0), table_of(cells, ids), preferred_element_type=jnp.float32
        )
        for a in range(3):
            low, high = a * rows_d, (a + 1) * rows_d
            value_a = value[low:high] + value[3 * rows_d + low:3 * rows_d + high]
            out_ref[0, a, pl.ds(d, 1), :] = jnp.sum(value_a * banded, axis=0, keepdims=True)
        return carry

    lax.fori_loop(0, bricks, gather, 0, unroll=4)

    def finish(r, carry):
        for i in range(len(pieces)):
            transfer(i, r).wait_send()
        return carry

    lax.fori_loop(0, n_row, finish, 0)


def body(n_row, n_col, send_cells, send_species, send_mix, send_counts, chi):
    species, domains, slots = send_mix.shape[1:]
    band = NZ // domains
    halves = 2 * n_row
    rows_d = species * band
    pieces = pieces_of(band)
    left, right, along_z = constants_of(species, band)
    rows_h = -(-2 * REACH * species // 8) * 8
    edge_rows = [n_col * n * species for _, _, n, _ in pieces]
    operands = (send_cells, send_species, send_mix, chi, left, right, along_z)
    grid = lambda rows: pltpu.VMEM((halves, n_col, rows, LANES), jnp.float32)
    return pl.pallas_call(
        functools.partial(membrane_kernel, n_row, n_col, band),
        out_shape=jax.ShapeDtypeStruct((1, 3, domains, slots), jnp.float32),
        in_specs=[pl.BlockSpec(memory_space=pltpu.SMEM)] + [pl.BlockSpec(memory_space=pl.ANY)] * 7,
        out_specs=pl.BlockSpec(memory_space=pltpu.VMEM),
        scratch_shapes=[pltpu.VMEM(operand.shape, operand.dtype) for operand in operands]
        + [pltpu.VMEM((n_row, rows, BX * BY), jnp.bfloat16) for rows in edge_rows] * 2
        + [pltpu.VMEM((rows, BX * BY), jnp.float32) for rows in edge_rows]
        + [pltpu.VMEM((species, domains, slots), jnp.float32)]
        + [grid(rows_d), grid(rows_d), grid(rows_h), grid(rows_h), grid(2 * rows_d)]
        + [pltpu.VMEM((4 * rows_d, along_z.shape[2]), jnp.bfloat16)]
        + [pltpu.VMEM((BX * BY, LANES), jnp.bfloat16)]
        + [
            pltpu.SemaphoreType.DMA((7,)),
            pltpu.SemaphoreType.DMA((len(pieces), n_row)),
            pltpu.SemaphoreType.DMA((len(pieces), n_row)),
        ],
        compiler_params=pltpu.CompilerParams(
            collective_id=0, has_side_effects=True, vmem_limit_bytes=56 * 2**20
        ),
        name="membrane",
    )(send_counts, *operands)


def solution(mesh):
    spec = P(("row", "col"))
    return jax.shard_map(
        functools.partial(body, mesh.shape["row"], mesh.shape["col"]),
        mesh=mesh,
        in_specs=(spec, spec, spec, spec, P()),
        out_specs=spec,
        check_vma=False,
    )
```

```python
import functools

import jax
import jax.numpy as jnp
import numpy as np
from jax import lax
from jax.experimental import pallas as pl
from jax.experimental.pallas import tpu as pltpu
from jax.sharding import PartitionSpec as P

BX = 16
BY = 16
NZ = 256
LANES = 128
HALF = LANES // BY
REACH = 3

raw_taps = (0.1353352832366127, 0.6065306597126334, 1.0, 0.6065306597126334, 0.1353352832366127)
tap_total = sum(raw_taps)
taps = tuple(t / tap_total for t in raw_taps)
rho_ref = 2.0
inv_kappa = 1.0


def pieces_of(band):
    out = []
    hop, left = 1, REACH
    while left > 0:
        n = min(band, left)
        out.append((hop, band - n, n, -(hop - 1) * band - n))
        out.append((-hop, 0, n, hop * band))
        left -= n
        hop += 1
    return out


def constants_of(species, band):
    pieces = pieces_of(band)
    rows_d = species * band
    rows_h = -(-2 * REACH * species // 8) * 8
    source = [(k, z) for k in range(species) for z in range(band)]
    source += [(k, at + p) for _, _, n, at in pieces for k in range(species) for p in range(n)]
    rows_m = -(-(rows_d + rows_h) // 16) * 16
    left = np.zeros((2 * rows_d, species), np.float32)
    right = np.zeros((species, rows_m), np.float32)
    along_z = np.zeros((2, 2 * rows_d, rows_m), np.float32)
    tap = lambda t: taps[t + 2] if -2 <= t <= 2 else 0.0
    for kind in range(2):
        for k in range(species):
            for z in range(band):
                i = kind * rows_d + k * band + z
                left[i, k] = 1.0
                for j, (l, at) in enumerate(source):
                    right[l, j] = 1.0
                    value = tap(at - z) if kind == 0 else tap(at - z - 1) - tap(at - z + 1)
                    along_z[0, i, j] = -0.5 * value * (0.5 / rho_ref) * float(k != l)
                    along_z[1, i, j] = -0.5 * value * (inv_kappa / rho_ref)
    return left, right, along_z


def exact(a, b, dims=(((1,), (0,)), ((), ()))):
    return lax.dot_general(a, b, dims, precision=lax.Precision.HIGHEST, preferred_element_type=jnp.float32)


def fill_weights(species_ref, mix_ref, wts):
    for k in range(wts.shape[0]):
        onehot = (species_ref[0] == k).astype(jnp.float32)
        wts[k] = (onehot + mix_ref[0, k].astype(jnp.float32)).astype(jnp.bfloat16).astype(jnp.float32)


def banded_of(cells, count, wts, d, first_z, band):
    slots = cells.shape[1]
    z = (cells & (NZ - 1)) - first_z
    z = jnp.where(lax.broadcasted_iota(jnp.int32, (1, slots), 1) < count, z, -1)
    hit = z == lax.broadcasted_iota(jnp.int32, (band, slots), 0)
    parts = [jnp.where(hit, wts[k, pl.ds(d, 1), :], 0.0) for k in range(wts.shape[0])]
    return jnp.concatenate(parts, axis=0)


def table_of(cells, ids):
    plane = lax.shift_right_logical(cells, NZ.bit_length() - 1).astype(jnp.float32).astype(jnp.bfloat16)
    one, none = jnp.ones((), jnp.bfloat16), jnp.zeros((), jnp.bfloat16)
    numbers = ids[...]
    parts = [
        jnp.where(plane[:, at:at + LANES] == numbers, one, none) for at in range(0, cells.shape[1], LANES)
    ]
    return jnp.concatenate(parts, axis=1)


def chunks_of(rows):
    return [(at, min(8, rows - at)) for at in range(0, rows, 8)]


def lane_of(rows):
    return lax.broadcasted_iota(jnp.int32, (rows, LANES), 1)


def lane_x_of(rows):
    return lax.shift_right_logical(lane_of(rows), BY.bit_length() - 1)


def lane_y_of(rows):
    return lane_of(rows) & (BY - 1)


def roll(value, shift):
    return pltpu.roll(value, shift % LANES, 1)


def moved_y(ahead, here, lane_y, t):
    if t > 0:
        return roll(jnp.where(lane_y < t, ahead, here), -t)
    return roll(jnp.where(lane_y >= BY + t, ahead, here), -t)


def moved_x(ahead, here, lane_x, t):
    if t > 0:
        return roll(jnp.where(lane_x < t, ahead, here), -t * BY)
    return roll(jnp.where(lane_x >= HALF + t, ahead, here), -t * BY)


def smoothed(moved, before, here, after, lane):
    one = moved(after, here, lane, 1) + moved(before, here, lane, -1)
    two = moved(after, here, lane, 2) + moved(before, here, lane, -2)
    return taps[2] * here + taps[3] * one + taps[4] * two


def smooth_y(src, r, q):
    n_col = src.shape[1]
    out = ([], [])
    for h in range(2):
        for at, size in chunks_of(src.shape[2]):
            lane_y = lane_y_of(size)
            before = src[2 * r + h, (q + n_col - 1) % n_col, at:at + size]
            after = src[2 * r + h, (q + 1) % n_col, at:at + size]
            here = src[2 * r + h, q, at:at + size]
            out[h].append(smoothed(moved_y, roll(before, -BY), here, roll(after, BY), lane_y))
    return out


def keep(dst, r, q, done):
    for h in range(2):
        for (at, size), value in zip(chunks_of(dst.shape[2]), done[h]):
            dst[2 * r + h, q, at:at + size] = value


def smooth_x(src, r, q):
    halves = src.shape[0]
    out = ([], [])
    for at, size in chunks_of(src.shape[2]):
        lane_x = lane_x_of(size)
        a, b = src[(2 * r + halves - 1) % halves, q, at:at + size], src[2 * r, q, at:at + size]
        c, d = src[2 * r + 1, q, at:at + size], src[(2 * r + 2) % halves, q, at:at + size]
        out[0].append(smoothed(moved_x, a, b, c, lane_x))
        out[1].append(smoothed(moved_x, b, c, d, lane_x))
    return out


def membrane_kernel(n_row, n_col, band, counts_ref, cells_hbm, species_hbm, mix_hbm, chi_hbm, left_hbm, right_hbm,
                    along_hbm, out_ref, *refs):
    pieces = pieces_of(band)
    held, refs = refs[:7], refs[7:]
    sends, refs = refs[:len(pieces)], refs[len(pieces):]
    recvs, refs = refs[:len(pieces)], refs[len(pieces):]
    stages, refs = refs[:len(pieces)], refs[len(pieces):]
    wts, raw, turned, edge_raw, edge_turned, fields, maps, ids, load_sem, send_sem, recv_sem = refs
    cells_ref, species_ref, mix_ref, chi_ref, left_ref, right_ref, along_ref = held
    count = wts.shape[0]
    rows_d, rows_h = count * band, edge_raw.shape[2]
    halves, rows_m = 2 * n_row, maps.shape[1]
    bricks = n_row * n_col
    me = lax.axis_index("row") * n_col + lax.axis_index("col")
    first_z = me * band

    loads = [
        pltpu.make_async_copy(src, dst, load_sem.at[i])
        for i, (src, dst) in enumerate(
            zip((cells_hbm, species_hbm, mix_hbm, chi_hbm, left_hbm, right_hbm, along_hbm), held)
        )
    ]
    for load in loads:
        load.start()

    def device_at(hop):
        there = (me + hop + bricks) % bricks
        return (there // n_col, there % n_col)

    barrier = pltpu.get_barrier_semaphore()
    for hop, _, _, _ in pieces:
        pl.semaphore_signal(barrier, inc=1, device_id=device_at(hop), device_id_type=pl.DeviceIdType.MESH)

    def transfer(i, r):
        return pltpu.make_async_remote_copy(
            src_ref=sends[i].at[r],
            dst_ref=recvs[i].at[r],
            send_sem=send_sem.at[i, r],
            recv_sem=recv_sem.at[i, r],
            device_id=device_at(pieces[i][0]),
            device_id_type=pl.DeviceIdType.MESH,
        )

    for load in loads[:3]:
        load.wait()
    fill_weights(species_ref, mix_ref, wts)
    ids[...] = lax.broadcasted_iota(jnp.int32, ids.shape, 0).astype(jnp.float32).astype(jnp.bfloat16)
    used = 2 * REACH * count
    if rows_h > used:
        edge_raw[:, :, used:] = jnp.zeros((halves, n_col, rows_h - used, LANES), jnp.float32)
    pl.semaphore_wait(barrier, len(pieces))

    def deposit(r, carry):
        for q in range(n_col):
            d = r * n_col + q
            cells = cells_ref[0, pl.ds(d, 1), :]
            banded = banded_of(cells, counts_ref[0, d], wts, d, first_z, band)
            tile = lax.dot_general(
                banded.astype(jnp.bfloat16), table_of(cells, ids), (((1,), (1,)), ((), ())),
                preferred_element_type=jnp.float32,
            )
            raw[2 * r, q] = tile[:, :LANES]
            raw[2 * r + 1, q] = tile[:, LANES:]
            for stage, (_, first, n, _) in zip(stages, pieces):
                for k in range(count):
                    to = (q * count + k) * n
                    stage[to:to + n, :] = tile[k * band + first:k * band + first + n]
        for i in range(len(pieces)):
            sends[i][r] = stages[i][...].astype(jnp.bfloat16)
            transfer(i, r).start()
        return carry

    lax.fori_loop(0, n_row, deposit, 0)

    for load in loads[3:]:
        load.wait()
    chi = chi_ref[...]
    mixing = exact(exact(left_ref[...], chi), right_ref[...])
    mixing += exact(exact(left_ref[...], chi, (((1,), (1,)), ((), ()))), right_ref[...])
    full = mixing * along_ref[0] + along_ref[1]
    high = full.astype(jnp.bfloat16)
    maps[:2 * rows_d] = high
    maps[2 * rows_d:] = (full - high.astype(jnp.float32)).astype(jnp.bfloat16)

    def inner_y(d, carry):
        r, q = d // n_col, d % n_col
        keep(turned, r, q, smooth_y(raw, r, q))
        return carry

    lax.fori_loop(0, bricks, inner_y, 0, unroll=2)

    def inner_x(d, carry):
        r, q = d // n_col, d % n_col
        keep(raw, r, q, smooth_x(turned, r, q))
        return carry

    lax.fori_loop(0, bricks, inner_x, 0, unroll=4)

    def edge_y(r, carry):
        for i in range(len(pieces)):
            transfer(i, r).wait_recv()
        got = [recv[r].astype(jnp.float32) for recv in recvs]
        for q in range(n_col):
            at = 0
            for part, (_, _, n, _) in zip(got, pieces):
                rows = n * count
                for h in range(2):
                    edge_raw[2 * r + h, q, at:at + rows] = part[q * rows:(q + 1) * rows, h * LANES:(h + 1) * LANES]
                at += rows

        def one(q, carry):
            keep(edge_turned, r, q, smooth_y(edge_raw, r, q))
            return carry

        return lax.fori_loop(0, n_col, one, carry, unroll=2)

    lax.fori_loop(0, n_row, edge_y, 0)

    def to_fields(d, carry):
        r, q = d // n_col, d % n_col
        done = []
        for h, edges in enumerate(smooth_x(edge_turned, r, q)):
            parts = [raw[2 * r + h, q]] + edges
            if rows_m > rows_d + rows_h:
                parts.append(jnp.zeros((rows_m - rows_d - rows_h, LANES), jnp.float32))
            done.append(jnp.concatenate(parts, axis=0))
        value = jnp.concatenate(done, axis=1)
        top = value.astype(jnp.bfloat16)
        rest = (value - top.astype(jnp.float32)).astype(jnp.bfloat16)
        first = jnp.dot(maps[...], top, preferred_element_type=jnp.float32)
        field = first[:2 * rows_d] + first[2 * rows_d:]
        field = field + jnp.dot(maps[:2 * rows_d], rest, preferred_element_type=jnp.float32)
        fields[2 * r, q] = field[:, :LANES]
        fields[2 * r + 1, q] = field[:, LANES:]
        return carry

    lax.fori_loop(0, bricks, to_fields, 0, unroll=8)

    def gather(d, carry):
        r, q = d // n_col, d % n_col
        grads = ([], [], [])
        for at, size in chunks_of(rows_d):
            lane_x, lane_y = lane_x_of(size), lane_y_of(size)
            sides = ([], [])
            for h in range(2):
                half = 2 * r + h
                here = fields[half, q, at:at + size]
                back, on = (fields[(half + step + halves) % halves, q, at:at + size] for step in (-1, 1))
                sides[0].append(moved_x(on, here, lane_x, 1) - moved_x(back, here, lane_x, -1))
                back, on = (fields[half, (q + step + n_col) % n_col, at:at + size] for step in (-1, 1))
                back, on = roll(back, -BY), roll(on, BY)
                sides[1].append(moved_y(on, here, lane_y, 1) - moved_y(back, here, lane_y, -1))
            for a in range(2):
                grads[a].append(jnp.concatenate(sides[a], axis=1))
        grads[2].append(
            jnp.concatenate([fields[2 * r, q, rows_d:], fields[2 * r + 1, q, rows_d:]], axis=1)
        )
        grad = jnp.concatenate(grads[0] + grads[1] + grads[2], axis=0)
        cells = cells_ref[0, pl.ds(d, 1), :]
        banded = banded_of(cells, counts_ref[0, d], wts, d, first_z, band)
        top = grad.astype(jnp.bfloat16)
        rest = (grad - top.astype(jnp.float32)).astype(jnp.bfloat16)
        value = jnp.dot(
            jnp.concatenate([top, rest], axis=0), table_of(cells, ids), preferred_element_type=jnp.float32
        )
        for a in range(3):
            low, high = a * rows_d, (a + 1) * rows_d
            value_a = value[low:high] + value[3 * rows_d + low:3 * rows_d + high]
            out_ref[0, a, pl.ds(d, 1), :] = jnp.sum(value_a * banded, axis=0, keepdims=True)
        return carry

    lax.fori_loop(0, bricks, gather, 0, unroll=8)

    def finish(r, carry):
        for i in range(len(pieces)):
            transfer(i, r).wait_send()
        return carry

    lax.fori_loop(0, n_row, finish, 0)


def body(n_row, n_col, send_cells, send_species, send_mix, send_counts, chi):
    species, domains, slots = send_mix.shape[1:]
    band = NZ // domains
    halves = 2 * n_row
    rows_d = species * band
    pieces = pieces_of(band)
    left, right, along_z = constants_of(species, band)
    rows_h = -(-2 * REACH * species // 8) * 8
    edge_rows = [n_col * n * species for _, _, n, _ in pieces]
    operands = (send_cells, send_species, send_mix, chi, left, right, along_z)
    grid = lambda rows: pltpu.VMEM((halves, n_col, rows, LANES), jnp.float32)
    return pl.pallas_call(
        functools.partial(membrane_kernel, n_row, n_col, band),
        out_shape=jax.ShapeDtypeStruct((1, 3, domains, slots), jnp.float32),
        in_specs=[pl.BlockSpec(memory_space=pltpu.SMEM)] + [pl.BlockSpec(memory_space=pl.ANY)] * 7,
        out_specs=pl.BlockSpec(memory_space=pltpu.VMEM),
        scratch_shapes=[pltpu.VMEM(operand.shape, operand.dtype) for operand in operands]
        + [pltpu.VMEM((n_row, rows, BX * BY), jnp.bfloat16) for rows in edge_rows] * 2
        + [pltpu.VMEM((rows, BX * BY), jnp.float32) for rows in edge_rows]
        + [pltpu.VMEM((species, domains, slots), jnp.float32)]
        + [grid(rows_d), grid(rows_d), grid(rows_h), grid(rows_h), grid(2 * rows_d)]
        + [pltpu.VMEM((4 * rows_d, along_z.shape[2]), jnp.bfloat16)]
        + [pltpu.VMEM((BX * BY, LANES), jnp.bfloat16)]
        + [
            pltpu.SemaphoreType.DMA((7,)),
            pltpu.SemaphoreType.DMA((len(pieces), n_row)),
            pltpu.SemaphoreType.DMA((len(pieces), n_row)),
        ],
        compiler_params=pltpu.CompilerParams(
            collective_id=0, has_side_effects=True, vmem_limit_bytes=56 * 2**20
        ),
        name="membrane",
    )(send_counts, *operands)


def solution(mesh):
    spec = P(("row", "col"))
    return jax.shard_map(
        functools.partial(body, mesh.shape["row"], mesh.shape["col"]),
        mesh=mesh,
        in_specs=(spec, spec, spec, spec, P()),
        out_specs=spec,
        check_vma=False,
    )
```
